128 devices in a mesh: rep: 16 (over y_hi, z, core), shard: 8 (over y_lo, x).
Axes of the slice: x: 4, y: 4 (y_hi: 2, y_lo: 2; y = y_hi * 2 + y_lo), z: 4, core: 2. Of those that a mesh axis runs over, the one named last changes fastest.
Arguments:
- tokens: bfloat16 [18432, 1088], P(('rep', 'shard')), may hold values from -6 to 6
- cotangent: bfloat16 [18432, 1088], P(('rep', 'shard')), may hold values from -6 to 6
- segments: int32 [18432], P('rep'), may hold values from 0 to 33, as said below
- gain_one: bfloat16 [2, 1088], P(None, 'shard'), may hold values from 0.5 to 1.5
- shift_one: bfloat16 [2, 1088], P(None, 'shard'), may hold values from -3 to 3
- w_qkv: bfloat16 [2, 1088, 3264], P(None, 'shard'), may hold values from -0.25 to 0.25
- bias_qv: bfloat16 [2, 2176], P(None, 'shard'), may hold values from -3 to 3
- w_out: bfloat16 [2, 1088, 1088], P(None, 'shard'), may hold values from -0.5 to 0.5
- bias_out: bfloat16 [2, 1088], P(None, 'shard'), may hold values from -3 to 3
- gain_two: bfloat16 [2, 1088], P(None, 'shard'), may hold values from 0.5 to 1.5
- shift_two: bfloat16 [2, 1088], P(None, 'shard'), may hold values from -3 to 3
- w_up: bfloat16 [2, 1088, 4352], P(None, 'shard'), may hold values from -0.1875 to 0.1875
- bias_up: bfloat16 [2, 4352], P(None, 'shard'), may hold values from -3 to 3
- w_down: bfloat16 [2, 4352, 1088], P(None, 'shard'), may hold values from -0.125 to 0.125
- bias_down: bfloat16 [2, 1088], P(None, 'shard'), may hold values from -3 to 3
Outputs:
- output: bfloat16 [18432, 1088], P(('rep', 'shard'))
- grad_tokens: bfloat16 [18432, 1088], P(('rep', 'shard'))
- grad_gain_one: float32 [2, 1088], P(None, 'shard')
- grad_shift_one: float32 [2, 1088], P(None, 'shard')
- grad_w_qkv: float32 [2, 1088, 3264], P(None, 'shard')
- grad_bias_qv: float32 [2, 2176], P(None, 'shard')
- grad_w_out: float32 [2, 1088, 1088], P(None, 'shard')
- grad_bias_out: float32 [2, 1088], P(None, 'shard')
- grad_gain_two: float32 [2, 1088], P(None, 'shard')
- grad_shift_two: float32 [2, 1088], P(None, 'shard')
- grad_w_up: float32 [2, 1088, 4352], P(None, 'shard')
- grad_bias_up: float32 [2, 4352], P(None, 'shard')
- grad_w_down: float32 [2, 4352, 1088], P(None, 'shard')
- grad_bias_down: float32 [2, 1088], P(None, 'shard')
The draws below stay inside these ranges and needn't reach their ends.
Inputs may be any that keep to these rules, and one draw needn't show every extreme that they name: `segments`: within each pack of 1152 tokens the sequence numbers start at 0, never fall and rise by at most one from token to token; every pack holds exactly 34 sequences; one holds exactly 1024 tokens and starts among the pack's first 129 positions, after at least one other sequence.
All inputs are finite; a program needn't handle non-finite values.
Results may differ from the reference program's by a relative error of at most 0.028.
Values may be sent and summed in bfloat16 or wider, within the bound.
No kernel may reach another device: no remote copies, remote signals or barrier semaphores. Data moves between devices by JAX's collectives and lax.ppermute only.
A program may use at most 256 MiB of HBM per device.

```python
import jax
import jax.numpy as jnp
from jax import lax

D = 1088
HEADS = 17
HEAD_DIM = 64
FF = 4352
LAYERS = 2
PACK = 1152
SLACK = 128
TOKENS = 18432


def pack_segments(key):
    short_count = SLACK // 4 + 1
    long_length = PACK - SLACK
    key_cuts, key_place = jax.random.split(key)
    order = jax.random.permutation(key_cuts, SLACK - 1)
    cut_places = order[:short_count - 1] + 1
    marks = jnp.zeros((SLACK,), jnp.int32).at[cut_places].set(1).at[0].set(1)
    short_ids = (jnp.cumsum(marks) - 1).astype(jnp.int32)
    placed = jax.random.randint(key_place, (), 1, short_count + 1)
    long_start = jnp.sum((short_ids < placed).astype(jnp.int32))
    position = jnp.arange(PACK, dtype=jnp.int32)
    before = short_ids[jnp.clip(position, 0, SLACK - 1)]
    after = short_ids[jnp.clip(position - long_length, 0, SLACK - 1)] + 1
    inside = (position >= long_start) & (position < long_start + long_length)
    return jnp.where(position < long_start, before, jnp.where(inside, placed, after)).astype(jnp.int32)


def draw_segments(key, part):
    key = jax.random.fold_in(key, 7)
    pack_count = TOKENS // PACK
    keys = jax.random.split(key, pack_count)
    return jax.vmap(pack_segments)(keys).reshape(TOKENS).astype(jnp.int32)


def shard_levels(own_key, dims, cuts, low, largest):
    factor_of, own = 1.0, jax.random.fold_in(own_key, 6)
    for dim, parts in cuts:
        draws = jnp.exp(jax.random.uniform(jax.random.fold_in(own, dim), (parts,), jnp.float32, low / len(cuts), largest / len(cuts)))
        factor_of = factor_of * jnp.repeat(draws, dims[dim] // parts).reshape([-1 if axis == dim else 1 for axis in range(len(dims))])
    return factor_of


def noise(stream_key, shape, spread, reach, cuts=(), kind=jnp.bfloat16):
    factor_of = shard_levels(stream_key, shape, cuts, -0.22, 0.18) if cuts else 1.0
    array = jax.random.normal(stream_key, shape, jnp.float32) * spread * factor_of
    return jnp.minimum(jnp.maximum(array, -reach), reach).astype(kind)


def setup_inputs(seed: int = 0) -> dict:
    arg_keys = jax.random.split(jax.random.key(seed), 16)
    return {
        "tokens": noise(arg_keys[0], (TOKENS, D), 1.0, 6.0, ((0, 128),)),
        "cotangent": noise(arg_keys[1], (TOKENS, D), 1.0, 6.0, ((0, 128),)),
        "segments": draw_segments(jax.random.fold_in(arg_keys[15], 71), 0),
        "gain_one": jnp.clip(1.0 + 0.1 * jax.random.normal(arg_keys[3], (LAYERS, D), jnp.float32), 0.5, 1.5).astype(jnp.bfloat16),
        "shift_one": noise(arg_keys[4], (LAYERS, D), 0.5, 3.0, ((1, 8),)),
        "w_qkv": noise(arg_keys[5], (LAYERS, D, 3 * D), (D // 2) ** -0.5, 0.25, ((1, 8),)),
        "bias_qv": noise(arg_keys[6], (LAYERS, 2 * D), 0.5, 3.0, ((1, 8),)),
        "w_out": noise(arg_keys[7], (LAYERS, D, D), (D // 8) ** -0.5, 0.5, ((1, 8),)),
        "bias_out": noise(arg_keys[8], (LAYERS, D), 0.5, 3.0, ((1, 8),)),
        "gain_two": jnp.clip(1.0 + 0.1 * jax.random.normal(arg_keys[9], (LAYERS, D), jnp.float32), 0.5, 1.5).astype(jnp.bfloat16),
        "shift_two": noise(arg_keys[10], (LAYERS, D), 0.5, 3.0, ((1, 8),)),
        "w_up": noise(arg_keys[11], (LAYERS, D, FF), D ** -0.5, 0.1875, ((1, 8),)),
        "bias_up": noise(arg_keys[12], (LAYERS, FF), 0.5, 3.0, ((1, 8),)),
        "w_down": noise(arg_keys[13], (LAYERS, FF, D), (FF // 2) ** -0.5, 0.125, ((1, 8),)),
        "bias_down": noise(arg_keys[14], (LAYERS, D), 0.5, 3.0, ((1, 8),)),
    }


@jax.custom_vjp
def low(v):
    return lax.optimization_barrier(v.astype(jnp.bfloat16)).astype(jnp.float32)

@jax.custom_vjp
def low_back(v):
    return v

def low_keep(v):
    return (low(v), None)

def low_pass(kept, grad):
    return (grad,)

def back_keep(v):
    return (v, None)

def back_low(kept, grad):
    return (low(grad),)
low.defvjp(low_keep, low_pass)
low_back.defvjp(back_keep, back_low)
HIGHEST_PRECISION = lax.Precision.HIGHEST
epsilon = 1e-05

def norm_rows(inputs, gain, shift):
    average = lax.optimization_barrier(jnp.mean(inputs, axis=-1, keepdims=True))
    centered = inputs - average
    variance = lax.optimization_barrier(jnp.mean(centered * centered, axis=-1, keepdims=True))
    return centered * lax.rsqrt(variance + epsilon) * gain + shift

def decoder_layer(stream, layer_params, segment):
    gain_a, shift_a, mix_weight, mix_bias, out_weight, out_bias, gain_b, shift_b, up_weight, up_bias, down_weight, down_bias = layer_params
    row_count = stream.shape[0]
    normed = low(norm_rows(stream, gain_a, shift_a))
    mixed = jnp.dot(normed, mix_weight, precision=HIGHEST_PRECISION)
    queries = low_back(low(mixed[:, :D] + mix_bias[:D]))
    key_rows = low_back(low(mixed[:, D:2 * D]))
    values = low_back(low(mixed[:, 2 * D:] + mix_bias[D:]))
    heads_q = queries.reshape(row_count, HEADS, HEAD_DIM)
    heads_k = key_rows.reshape(row_count, HEADS, HEAD_DIM)
    heads_v = values.reshape(row_count, HEADS, HEAD_DIM)
    places = jnp.arange(row_count, dtype=jnp.int32)
    allowed = (segment[:, None] == segment[None, :]) & (places[None, :] <= places[:, None])
    scores = low_back(jnp.einsum('thd,shd->hts', heads_q, heads_k, precision=HIGHEST_PRECISION) / jnp.sqrt(jnp.float32(HEAD_DIM)))
    scores = jnp.where(allowed[None], scores, -1e+30)
    highest = lax.optimization_barrier(jnp.max(scores, axis=-1, keepdims=True))
    exponent = jnp.exp(scores - highest)
    probability = exponent / lax.optimization_barrier(jnp.sum(exponent, axis=-1, keepdims=True))
    weights = low(probability)
    attended = jnp.einsum('hts,shd->thd', weights, heads_v, precision=HIGHEST_PRECISION).reshape(row_count, D)
    attended = low_back(low(attended))
    stream_mid = stream + low_back(jnp.dot(attended, out_weight, precision=HIGHEST_PRECISION) + out_bias)
    normed_b = low(norm_rows(stream_mid, gain_b, shift_b))
    up_value = low_back(jnp.dot(normed_b, up_weight, precision=HIGHEST_PRECISION) + up_bias)
    active = low(jax.nn.gelu(up_value, approximate=True))
    return stream_mid + low_back(jnp.dot(active, down_weight, precision=HIGHEST_PRECISION) + down_bias)

def reference(tokens, cotangent, segments, gain_one, shift_one, w_qkv, bias_qv, w_out, bias_out, gain_two, shift_two, w_up, bias_up, w_down, bias_down):
    params = tuple((member.astype(jnp.float32) for member in (gain_one, shift_one, w_qkv, bias_qv, w_out, bias_out, gain_two, shift_two, w_up, bias_up, w_down, bias_down)))
    stream_packs = tokens.astype(jnp.float32).reshape(-1, PACK, D)
    cotangent_packs = cotangent.astype(jnp.float32).reshape(-1, PACK, D)
    segment_packs = segments.reshape(-1, PACK)

    def forward(stream, weights_all, segment):
        for depth in range(LAYERS):
            stream = decoder_layer(stream, tuple((member[depth] for member in weights_all)), segment)
        return stream

    def visit_pack(totals, element):
        stream, grad_out, segment = element
        result, pullback = jax.vjp(lambda state, weights_all: forward(state, weights_all, segment), stream, params)
        grad_in, grad_params = pullback(grad_out)
        totals = tuple((running + latest for running, latest in zip(totals, grad_params)))
        return (totals, (result, grad_in))
    zeros = tuple((jnp.zeros_like(member) for member in params))
    totals, (results, grads_in) = lax.scan(visit_pack, zeros, (stream_packs, cotangent_packs, segment_packs))
    return (results.reshape(-1, D).astype(jnp.bfloat16), grads_in.reshape(-1, D).astype(jnp.bfloat16), totals[0], totals[1], totals[2], totals[3], totals[4], totals[5], totals[6], totals[7], totals[8], totals[9], totals[10], totals[11])
```

```python
import functools
import math

import jax
import jax.numpy as jnp
import numpy as np
from jax import lax
from jax.experimental import pallas as pl
from jax.experimental.pallas import tpu as pltpu
from jax.sharding import Mesh
from jax.sharding import PartitionSpec as P

HEADS = 17
HEAD_DIM = 64
LAYERS = 2
D = 1088
FF = 4352
ROWS = 144
PACK = 1152
SCALE = 1.0 / math.sqrt(HEAD_DIM)
EPS = 1e-05
ALL = ("yh", "z", "c", "yl", "x")
REP = ("yh", "z", "c")
SHARD = ("yl", "x")
BF = jnp.bfloat16
F32 = jnp.float32


def build_perm(move):
    index = np.arange(128).reshape(2, 4, 2, 2, 4)
    pairs = []
    for yh in range(2):
        for z in range(4):
            for c in range(2):
                for yl in range(2):
                    for x in range(4):
                        target = move(x, 2 * yh + yl, z, c)
                        if target is None:
                            continue
                        tx, ty, tz, tc = (value % size for value, size in zip(target, (4, 4, 4, 2)))
                        pairs.append(
                            (int(index[yh, z, c, yl, x]), int(index[ty // 2, tz, tc, ty % 2, tx]))
                        )
    return pairs


NEAR_X = build_perm(lambda x, y, z, c: (x + 1 if c == 0 else x - 1, y, z, c))
FAR_X = build_perm(lambda x, y, z, c: (x + 2, y, z, c) if c == 1 else None)
NEAR_Y = build_perm(lambda x, y, z, c: (x, y + 1 if c == 0 else y - 1, z, c))
OTHER_CORE = build_perm(lambda x, y, z, c: (x, y, z, 1 - c))


def move(array, pairs):
    return lax.ppermute(array, ALL, pairs)


def exchange(array, axes):
    return lax.all_to_all(array, axes, 0, 0, tiled=True)


def norm_rows(inputs, gain, shift):
    average = jnp.mean(inputs, axis=-1, keepdims=True)
    centered = inputs - average
    variance = jnp.mean(centered * centered, axis=-1, keepdims=True)
    return centered * lax.rsqrt(variance + EPS) * gain + shift


def gelu_tanh(inputs):
    return jax.nn.gelu(inputs, approximate=True)


def gather_blocks(own, core):
    near = move(own, NEAR_X)
    far = move(own, FAR_X)
    first = jnp.where(core == 0, own, far)
    first_y = move(first, NEAR_Y)
    near_y = move(near, NEAR_Y)
    blocks = [
        (0, 0, 2, first),
        (0, 3, 1, near),
        (1, 0, 2, first_y),
        (1, 3, 1, near_y),
        (0, 2, 0, move(first, OTHER_CORE)),
        (0, 1, 3, move(near, OTHER_CORE)),
        (1, 2, 0, move(first_y, OTHER_CORE)),
        (1, 1, 3, move(near_y, OTHER_CORE)),
    ]
    return blocks, (near, far)


def after(array, earlier):
    return lax.optimization_barrier((array, earlier))[0]


def gather_halves(zero, one, core):
    return lax.all_gather(core_half(core, zero, one), SHARD, axis=0, tiled=True)


def join_halves(half):
    both = exchange(jnp.broadcast_to(half[None], (2,) + half.shape), "c")
    return both[0], both[1]


def assemble(blocks, pick, core, y_low, x_pos, shape):
    whole = jnp.zeros((8,) + shape, BF)
    for other, offset_zero, offset_one, block in blocks:
        x_from = lax.rem(x_pos + jnp.where(core == 0, offset_zero, offset_one), 4)
        y_from = y_low if other == 0 else 1 - y_low
        whole = lax.dynamic_update_slice(
            whole, pick(block)[None], (4 * y_from + x_from,) + (0,) * len(shape)
        )
    return whole


BLOCK = 128
DOT_NT = (((1,), (1,)), ((), ()))
DOT_TN = (((0,), (0,)), ((), ()))


def dot_f32(left, right, dims=(((1,), (0,)), ((), ()))):
    return lax.dot_general(left, right, dims, preferred_element_type=F32)


def softmax_rows(queries, keys, allowed):
    scores = jnp.where(allowed, dot_f32(queries, keys, DOT_NT) * SCALE, -1e30)
    highest = jnp.max(scores, axis=-1, keepdims=True)
    exponent = jnp.exp(scores - highest)
    return exponent / jnp.sum(exponent, axis=-1, keepdims=True)


def block_mask(seg_col, seg_row, first_row, rows, keys):
    row = lax.broadcasted_iota(jnp.int32, (rows, keys), 0) + first_row
    col = lax.broadcasted_iota(jnp.int32, (rows, keys), 1)
    return (seg_col == seg_row) & (col <= row)


def attend_kernel(place, qkv, q_last, seg_col, seg_row, seg_own, out, out_last):
    for step in range(PACK // BLOCK):
        start, keys = step * BLOCK, (step + 1) * BLOCK
        allowed = block_mask(
            seg_col[start:keys, :], seg_row[:, 0:keys], start, BLOCK, keys
        )
        for head in range(2):
            lane = head * 64
            weights = softmax_rows(
                qkv[start:keys, lane : lane + 64], qkv[0:keys, 128 + lane : 192 + lane], allowed
            ).astype(BF)
            out[start:keys, lane : lane + 64] = dot_f32(
                weights, qkv[0:keys, 256 + lane : 320 + lane]
            ).astype(BF)
    allowed = block_mask(seg_own[...], seg_row[...], place[0], ROWS, PACK)
    weights = softmax_rows(q_last[:, 0:64], qkv[:, 384:448], allowed).astype(BF)
    out_last[...] = dot_f32(weights, qkv[:, 448:512]).astype(BF)


def attend_back_kernel(
    place, qkv, q_last, seg_col, seg_row, seg_own, dout, dout_last, dqkv, dq_last, dk, dv
):
    def pull(queries, keys, values, grad, allowed):
        probability = softmax_rows(queries, keys, allowed)
        grad_prob = dot_f32(grad, values, DOT_NT)
        inner = jnp.sum(grad_prob * probability, axis=-1, keepdims=True)
        grad_scores = (probability * (grad_prob - inner)).astype(BF)
        weights = probability.astype(BF)
        return (
            dot_f32(grad_scores, keys) * SCALE,
            dot_f32(grad_scores, queries, DOT_TN) * SCALE,
            dot_f32(weights, grad, DOT_TN),
        )

    dk[...] = jnp.zeros_like(dk)
    dv[...] = jnp.zeros_like(dv)
    for step in range(PACK // BLOCK):
        start, keys = step * BLOCK, (step + 1) * BLOCK
        allowed = block_mask(
            seg_col[start:keys, :], seg_row[:, 0:keys], start, BLOCK, keys
        )
        for head in range(2):
            lane = head * 64
            part_q, part_k, part_v = pull(
                qkv[start:keys, lane : lane + 64],
                qkv[0:keys, 128 + lane : 192 + lane],
                qkv[0:keys, 256 + lane : 320 + lane],
                dout[start:keys, lane : lane + 64],
                allowed,
            )
            dqkv[start:keys, lane : lane + 64] = part_q.astype(BF)
            dk[0:keys, lane : lane + 64] += part_k
            dv[0:keys, lane : lane + 64] += part_v
    dqkv[:, 128:256] = dk[...].astype(BF)
    dqkv[:, 256:384] = dv[...].astype(BF)
    allowed = block_mask(seg_own[...], seg_row[...], place[0], ROWS, PACK)
    part_q, part_k, part_v = pull(
        q_last[:, 0:64], qkv[:, 384:448], qkv[:, 448:512], dout_last[:, 0:64], allowed
    )
    dq_last[...] = part_q.astype(BF)
    dqkv[:, 384:448] = part_k.astype(BF)
    dqkv[:, 448:512] = part_v.astype(BF)


VMEM = pl.BlockSpec(memory_space=pltpu.VMEM)
SMEM = pl.BlockSpec(memory_space=pltpu.SMEM)


def attend(place, qkv, q_last, segs):
    return pl.pallas_call(
        attend_kernel,
        out_shape=(
            jax.ShapeDtypeStruct((PACK, 128), BF),
            jax.ShapeDtypeStruct((ROWS, 64), BF),
        ),
        in_specs=[SMEM] + [VMEM] * 5,
        out_specs=(VMEM, VMEM),
        compiler_params=pltpu.CompilerParams(vmem_limit_bytes=32 * 1024 * 1024),
        cost_estimate=pl.CostEstimate(flops=900_000_000, bytes_accessed=2_500_000, transcendentals=1_700_000),
        name="attend",
    )(place, qkv, q_last, *segs)


def attend_back(place, qkv, q_last, segs, dout, dout_last):
    return pl.pallas_call(
        attend_back_kernel,
        out_shape=(
            jax.ShapeDtypeStruct((PACK, 512), BF),
            jax.ShapeDtypeStruct((ROWS, 64), BF),
        ),
        in_specs=[SMEM] + [VMEM] * 7,
        out_specs=(VMEM, VMEM),
        scratch_shapes=[pltpu.VMEM((PACK, 128), F32)] * 2,
        compiler_params=pltpu.CompilerParams(vmem_limit_bytes=32 * 1024 * 1024),
        cost_estimate=pl.CostEstimate(flops=2_200_000_000, bytes_accessed=4_000_000, transcendentals=1_700_000),
        name="attend_back",
    )(place, qkv, q_last, *segs, dout, dout_last)


def by_head_pair(array):
    return array.reshape(ROWS, 8, 128).transpose(1, 0, 2)


def from_head_pair(array):
    return array.transpose(1, 0, 2).reshape(ROWS, 1024)


def times(left, weight):
    products = [jnp.dot(left, part, preferred_element_type=F32) for part in weight]
    return products[0] if len(products) == 1 else jnp.concatenate(products, axis=1)


def times_back(right, weight):
    total, start = None, 0
    for part in weight:
        product = dot_f32(right[:, start : start + part.shape[1]], part, DOT_NT)
        total = product if total is None else total + product
        start += part.shape[1]
    return total


def forward_attention(stream, small, big, place, segs):
    gain_a, shift_a, mix_bias, out_bias = small[:4]
    mix_weight, out_weight = big[:2]
    normed = norm_rows(stream, gain_a, shift_a).astype(BF)
    mixed = times(normed, mix_weight)
    queries = (mixed[:, :D] + mix_bias[:D]).astype(BF)
    key_rows = mixed[:, D : 2 * D].astype(BF)
    values = (mixed[:, 2 * D :] + mix_bias[D:]).astype(BF)
    last = jnp.concatenate([key_rows[:, 1024:], values[:, 1024:]], axis=1)
    send = jnp.concatenate(
        [
            by_head_pair(queries[:, :1024]),
            by_head_pair(key_rows[:, :1024]),
            by_head_pair(values[:, :1024]),
            jnp.broadcast_to(last[None], (8, ROWS, 128)),
        ],
        axis=2,
    )
    qkv = exchange(send, SHARD).reshape(PACK, 512)
    q_last = queries[:, 1024:]
    out, out_last = attend(place, qkv, q_last, segs)
    attended = jnp.concatenate(
        [from_head_pair(exchange(out.reshape(8, ROWS, 128), SHARD)), out_last], axis=1
    )
    stream_mid = stream + times(attended, out_weight) + out_bias
    return (stream, normed, qkv, q_last, attended), stream_mid


def forward_feed(stream_mid, small, big):
    gain_b, shift_b, up_bias, down_bias = small[4:]
    up_weight, down_weight = big[2:]
    normed_b = norm_rows(stream_mid, gain_b, shift_b).astype(BF)
    up_value = times(normed_b, up_weight) + up_bias
    active = gelu_tanh(up_value).astype(BF)
    result = stream_mid + times(active, down_weight) + down_bias
    return (stream_mid, normed_b, up_value, active), result


def both_cores(array):
    if array.shape[1] > D:
        return exchange(jnp.concatenate([array, array], axis=0), "c")
    return lax.all_gather(array, "c", axis=0, tiled=True)


def swap_halves(zero, one):
    return exchange(jnp.concatenate([zero, one], axis=0), "c")


def grad_pair(pieces):
    grads = [dot_f32(left, right, DOT_TN).astype(BF) for left, right in pieces]
    return grads[0] if len(grads) == 1 else jnp.concatenate(grads, axis=1)


def core_half(core, zero, one):
    return jnp.where(core == 0, zero, one)


def as_lanes(part):
    return part.reshape(136, FF // 2)


class SlowSum:
    def __init__(self):
        self.parts = []

    def add(self, pieces):
        self.parts.append(
            lax.psum_scatter(grad_pair(pieces), SHARD, scatter_dimension=0, tiled=True)
        )

    def finish(self, array):
        array, parts = lax.optimization_barrier((array, self.parts))
        joined = jnp.concatenate([as_lanes(part) for part in parts], axis=1)
        joined = lax.psum(joined, ("yh", "z"))
        joined = exchange(jnp.broadcast_to(joined[None], (2, 136, 3 * FF // 2)), "c")
        self.done = [joined[:, :, k * (FF // 2) : (k + 1) * (FF // 2)] for k in range(3)]
        return array


class FastSum:
    def __init__(self, core, y_low, waiting):
        self.y_low = y_low
        self.waiting = waiting
        self.sent = []
        self.parts = []

    def add(self, pieces):
        split = []
        for left, right in pieces:
            half = left.shape[1] // 2
            first, second = left[:, :half], left[:, half:]
            split.append(
                (
                    jnp.where(self.y_low == 0, second, first),
                    jnp.where(self.y_low == 0, first, second),
                    right,
                )
            )
        arrived = move(grad_pair([(other, right) for other, own, right in split]), NEAR_Y)
        self.sent.append(([(own, right) for other, own, right in split], arrived))

    def advance(self, array):
        array, arrived = lax.optimization_barrier((array, [item[1] for item in self.sent]))
        for (own, _), came in zip(self.sent, arrived):
            summed = [dot_f32(left, right, DOT_TN) for left, right in own]
            summed = summed[0] if len(summed) == 1 else jnp.concatenate(summed, axis=1)
            summed = (summed + came.astype(F32)).astype(BF)
            spread = exchange(summed, "x")
            self.parts.append(spread)
        self.sent = []
        return array

    def total(self, parts):
        summed = []
        for part in parts:
            rows = part.shape[0] // 4
            summed.append(
                as_lanes(jnp.sum(part.reshape(4, rows, -1).astype(F32), axis=0).astype(BF))
            )
        lanes = len(summed) * (FF // 2)
        wide = -(-lanes // 1024) * 1024
        summed.append(jnp.zeros((136, wide - lanes), BF))
        joined = jnp.concatenate(summed, axis=1)
        piece = wide // 8
        joined = joined.reshape(136, 8, piece).transpose(1, 0, 2)
        arrived = exchange(joined, ("yh", "z"))
        total = jnp.sum(arrived.astype(F32), axis=0).astype(BF)
        spread = exchange(jnp.broadcast_to(total[None], (16, 136, piece)), REP)
        spread = spread.reshape(8, 2, 136, piece).transpose(1, 2, 0, 3).reshape(2, 136, wide)
        return [spread[:, :, k * (FF // 2) : (k + 1) * (FF // 2)] for k in range(len(parts))]


def backward_layer(gradient, small, big, retained, place, segs, core, sums):
    gain_a, shift_a, mix_bias, out_bias, gain_b, shift_b, up_bias, down_bias = small
    mix_weight, out_weight, up_weight, down_weight = big
    stream, normed, qkv, q_last, attended, stream_mid, normed_b, up_value, active = retained
    fast = isinstance(sums, FastSum)
    grad_branch = gradient.astype(BF)
    grad_active = times_back(grad_branch, down_weight)
    gelu_pull = jax.vjp(gelu_tanh, up_value)[1]
    grad_up = gelu_pull(grad_active)[0].astype(BF)

    branch_both = both_cores(grad_branch)
    sums.add(
        [(both_cores(active), core_half(core, branch_both[:, : D // 2], branch_both[:, D // 2 :]))]
    )
    grad_normed_b = times_back(grad_up, up_weight)
    up_both = swap_halves(grad_up[:, : FF // 2], grad_up[:, FF // 2 :])
    sums.add([(both_cores(normed_b), up_both)])

    norm_pull_b = jax.vjp(norm_rows, stream_mid, gain_b, shift_b)[1]
    grad_mid_norm, grad_gain_b, grad_shift_b = norm_pull_b(grad_normed_b)
    grad_mid = gradient + grad_mid_norm
    grad_attn = grad_mid.astype(BF)
    grad_attended = times_back(grad_attn, out_weight).astype(BF)
    dout = exchange(by_head_pair(grad_attended[:, :1024]), SHARD).reshape(PACK, 128)
    if fast:
        dout = sums.advance(dout)
    dqkv, dq_last = attend_back(place, qkv, q_last, segs, dout, grad_attended[:, 1024:])
    arrived = exchange(dqkv.reshape(8, ROWS, 512), SHARD)
    if fast:
        arrived, sums.parts = lax.optimization_barrier((arrived, sums.parts))
        down_sum, up_sum = sums.total(sums.parts)
        sums.parts = []
    last = jnp.sum(arrived[:, :, 384:].astype(F32), axis=0).astype(BF)
    grad_queries = jnp.concatenate([from_head_pair(arrived[:, :, 0:128]), dq_last], axis=1)
    grad_keys = jnp.concatenate([from_head_pair(arrived[:, :, 128:256]), last[:, :64]], axis=1)
    grad_values = jnp.concatenate([from_head_pair(arrived[:, :, 256:384]), last[:, 64:]], axis=1)
    grad_mixed = jnp.concatenate([grad_queries, grad_keys, grad_values], axis=1)

    if fast:
        grad_mixed = sums.waiting.finish(grad_mixed)
    normed_both = both_cores(normed)
    attended_both = both_cores(attended)
    right = swap_halves(
        grad_mixed[:, : 2 * D], jnp.concatenate([grad_values, grad_attn], axis=1)
    )
    sums.add(
        [
            (normed_both, right[:, :D]),
            (core_half(core, normed_both, attended_both), right[:, D:]),
        ]
    )
    grad_normed = times_back(grad_mixed, mix_weight)
    norm_pull_a = jax.vjp(norm_rows, stream, gain_a, shift_a)[1]
    grad_in_norm, grad_gain_a, grad_shift_a = norm_pull_a(grad_normed)
    grad_in = grad_mid + grad_in_norm
    if fast:
        sums.advance(dout)
        owned_big = (sums.total(sums.parts)[0], up_sum, down_sum)
    else:
        owned_big = None
    small_grads = (
        grad_gain_a,
        grad_shift_a,
        jnp.concatenate(
            [jnp.sum(grad_queries.astype(F32), axis=0), jnp.sum(grad_values.astype(F32), axis=0)]
        ),
        jnp.sum(grad_attn.astype(F32), axis=0),
        grad_gain_b,
        grad_shift_b,
        jnp.sum(grad_up.astype(F32), axis=0),
        jnp.sum(grad_branch.astype(F32), axis=0),
    )
    small_grads = jnp.concatenate([vector.reshape(8, -1) for vector in small_grads], axis=1)
    return grad_in, owned_big, small_grads


SMALL_WIDTHS = (136, 136, 272, 136, 136, 136, 544, 136)
SMALL = sum(SMALL_WIDTHS)
SMALL_EDGES = [sum(SMALL_WIDTHS[:index]) for index in range(9)]


def body(
    tokens,
    cotangent,
    segments,
    gain_one,
    shift_one,
    w_qkv,
    bias_qv,
    w_out,
    bias_out,
    gain_two,
    shift_two,
    w_up,
    bias_up,
    w_down,
    bias_down,
):
    core = lax.axis_index("c")
    y_low = lax.axis_index("yl")
    x_pos = lax.axis_index("x")
    member = 4 * y_low + x_pos
    place = (member * ROWS).astype(jnp.int32).reshape(1)
    seg_own = lax.dynamic_slice_in_dim(segments, member * ROWS, ROWS)
    segs = (segments[:, None], segments[None, :], seg_own[:, None])

    vectors = (gain_one, shift_one, bias_qv, bias_out, gain_two, shift_two, bias_up, bias_down)
    own_small = jnp.concatenate(vectors, axis=1)
    all_small = exchange(jnp.broadcast_to(own_small[None], (8, LAYERS, SMALL)), SHARD)
    smalls = []
    for depth in range(LAYERS):
        smalls.append(
            tuple(
                all_small[:, depth, SMALL_EDGES[k] : SMALL_EDGES[k + 1]].reshape(-1).astype(F32)
                for k in range(8)
            )
        )

    put = functools.partial(assemble, core=core, y_low=y_low, x_pos=x_pos)
    blocks, came = gather_blocks(jnp.concatenate([w_qkv[0], w_out[0]], axis=1), core)
    mix = put(blocks, lambda b: b[:, : 3 * D], shape=(136, 3 * D)).reshape(D, 3 * D)
    out = put(blocks, lambda b: b[:, 3 * D :], shape=(136, D)).reshape(D, D)
    later = after((w_qkv[1], w_out[1], w_up[1], w_down[1]), came)
    blocks, came = gather_blocks(after(w_up[0], came), core)
    up = put(blocks, lambda b: b, shape=(136, FF)).reshape(D, FF)
    blocks, came = gather_blocks(after(w_down[0], came), core)
    down = put(blocks, lambda b: b, shape=(544, D)).reshape(FF, D)
    bigs = [((mix,), (out,), (up,), (down,))]
    halves = [
        gather_halves(
            later[0][:, : 2 * D], jnp.concatenate([later[0][:, 2 * D :], later[1]], axis=1), core
        ),
        gather_halves(later[2][:, : FF // 2], later[2][:, FF // 2 :], core),
        gather_halves(later[3][:, : D // 2], later[3][:, D // 2 :], core),
    ]

    stream = tokens.astype(F32)
    stored = []
    retained, mid = forward_attention(stream, smalls[0], bigs[0], place, segs)
    mid, halves[0] = lax.optimization_barrier((mid, halves[0]))
    zero, one = join_halves(halves[0])
    rest, stream = forward_feed(mid, smalls[0], bigs[0])
    stored.append(retained + rest)
    stream, halves[1] = lax.optimization_barrier((stream, halves[1]))
    second = [(zero, one[:, :D]), (one[:, D:],), join_halves(halves[1])]
    retained, mid = forward_attention(stream, smalls[1], second, place, segs)
    mid, halves[2] = lax.optimization_barrier((mid, halves[2]))
    second.append(join_halves(halves[2]))
    rest, stream = forward_feed(mid, smalls[1], second)
    stored.append(retained + rest)
    bigs.append(second)
    output = stream.astype(BF)

    gradient = cotangent.astype(F32)
    owned, small_grads = [None] * LAYERS, [None] * LAYERS
    slow = SlowSum()
    fast = FastSum(core, y_low, slow)
    for depth, sums in ((1, slow), (0, fast)):
        gradient, owned[depth], small_grads[depth] = backward_layer(
            gradient, smalls[depth], bigs[depth], stored[depth], place, segs, core, sums
        )
    down_sum, up_sum, mix_sum = slow.done
    owned[1] = (mix_sum, up_sum, down_sum)

    small_sum = jnp.sum(
        exchange(jnp.stack(small_grads, axis=1), SHARD).reshape(8, LAYERS, SMALL), axis=0
    )
    small_sum = jnp.sum(
        exchange(jnp.broadcast_to(small_sum[None], (16, LAYERS, SMALL)), REP), axis=0
    )
    small_out = [small_sum[:, SMALL_EDGES[k] : SMALL_EDGES[k + 1]] for k in range(8)]

    def stack(build):
        return jnp.stack([build(*owned[depth]) for depth in range(LAYERS)]).astype(F32)

    grad_qkv = stack(lambda mix, up, down: jnp.concatenate([mix[0], mix[1, :, :D]], axis=1))
    grad_out = stack(lambda mix, up, down: mix[1, :, D:])
    grad_up = stack(lambda mix, up, down: jnp.concatenate([up[0], up[1]], axis=1))
    grad_down = stack(lambda mix, up, down: jnp.concatenate([half.reshape(544, D // 2) for half in down], axis=1))
    return (
        output,
        gradient.astype(BF),
        small_out[0],
        small_out[1],
        grad_qkv,
        small_out[2],
        grad_out,
        small_out[3],
        small_out[4],
        small_out[5],
        grad_up,
        small_out[6],
        grad_down,
        small_out[7],
    )


def solution(mesh):
    fine = Mesh(mesh.devices.reshape(2, 4, 2, 2, 4), ALL)
    rows = P(ALL, None)
    vector = P(None, SHARD)
    matrix = P(None, SHARD, None)
    in_specs = (
        rows,
        rows,
        P(REP),
        vector,
        vector,
        matrix,
        vector,
        matrix,
        vector,
        vector,
        vector,
        matrix,
        vector,
        matrix,
        vector,
    )
    out_specs = (rows, rows) + in_specs[3:]
    return jax.shard_map(body, mesh=fine, in_specs=in_specs, out_specs=out_specs, check_vma=False)
```
